256 devices in a mesh: dp: 16 (over x_hi, z), expert: 16 (over y, x_lo, core).
Axes of the slice: x: 4 (x_hi: 2, x_lo: 2; x = x_hi * 2 + x_lo), y: 4, z: 8, core: 2. Of those that a mesh axis runs over, the one named last changes fastest.
Arguments:
- tokens: bfloat16 [65536, 4096], P(('dp', 'expert')), may hold values from -6 to 6
- chosen: int32 [256, 16, 32], P(('dp', 'expert')), may hold values from 0 to 255, as said below
- gates: float32 [256, 16, 32], P(('dp', 'expert')), may hold values from 0.25 to 1
- w_gate: bfloat16 [16, 4096, 768], P('expert', 'dp'), may hold values from -0.09375 to 0.09375
- w_up: bfloat16 [16, 4096, 768], P('expert', 'dp'), may hold values from -0.09375 to 0.09375
- w_down: bfloat16 [16, 768, 4096], P('expert', None, 'dp'), may hold values from -0.21875 to 0.21875
Outputs:
- layer_out: bfloat16 [65536, 4096], P(('dp', 'expert'))
The draws below stay inside these ranges and needn't reach their ends.
Inputs may be any that keep to these rules, and one draw needn't show every extreme that they name: `chosen`: for each slab and expert the 32 picked rows are distinct rows of the slab; every expert picks exactly 32 rows in every slab.
All inputs are finite; a program needn't handle non-finite values.
Results may differ from the reference program's by a relative error of at most 0.0049.
Values may be sent and summed in bfloat16 or wider, within the bound.
A program may use at most 128 MiB of HBM per device.

```python
import jax
import jax.numpy as jnp
from jax import lax

D = 4096
H = 768
TOK_DEV = 256
EXPERTS = 16
PER = 32
SLABS = 256
TOKENS = 65536


def draw_chosen(key, part):
    all_keys = jax.random.split(key, SLABS * EXPERTS)

    def pick_one(one_key):
        return jax.random.permutation(one_key, TOK_DEV)[:PER]
    picks = jax.vmap(pick_one)(all_keys)
    return picks.reshape(SLABS, EXPERTS, PER).astype(jnp.int32)


def shard_levels(rng, extent, cuts, least, top_value):
    def one(position, blocks):
        draws = jax.random.uniform(jax.random.fold_in(jax.random.fold_in(rng, 6), position), (blocks,), jnp.float32, least / len(cuts), top_value / len(cuts))
        return jnp.repeat(jnp.exp(draws), extent[position] // blocks).reshape((-1,) + (1,) * (len(extent) - position - 1))

    loudness = one(*cuts[0])
    for cut in cuts[1:]:
        loudness = loudness * one(*cut)
    return loudness


def centred(own_key, dims, scale, limit, cuts=(), held_as=jnp.bfloat16):
    array = jax.random.normal(own_key, dims, jnp.float32) * scale
    if len(cuts) > 0:
        array = shard_levels(own_key, dims, cuts, -0.22, 0.18) * array
    return jnp.clip(array, min=-limit, max=limit).astype(held_as)


def setup_inputs(seed: int = 0) -> dict:
    splits = jax.random.split(jax.random.key(seed), 7)
    tokens = centred(splits[0], (TOKENS, D), 1.0, 6.0, ((0, 256),))
    chosen = draw_chosen(jax.random.fold_in(splits[6], 71), 0)
    gates = jnp.clip(0.25 + 0.75 * jax.random.uniform(splits[2], (SLABS, EXPERTS, PER), jnp.float32) ** shard_levels(splits[2], (SLABS, EXPERTS, PER), ((0, 256),), -0.2, 0.2), 0.25, 1.0)
    w_gate = centred(splits[3], (EXPERTS, D, H), D ** -0.5, 0.09375, ((0, 16), (1, 16)))
    w_up = centred(splits[4], (EXPERTS, D, H), D ** -0.5, 0.09375, ((0, 16), (1, 16)))
    w_down = centred(splits[5], (EXPERTS, H, D), H ** -0.5, 0.21875, ((0, 16), (2, 16)))
    return {"tokens": tokens, "chosen": chosen, "gates": gates, "w_gate": w_gate, "w_up": w_up, "w_down": w_down}


def reference(tokens, chosen, gates, w_gate, w_up, w_down):
    slab_count = chosen.shape[0]
    model_width = tokens.shape[1]
    slab_base = (jnp.arange(slab_count, dtype=jnp.int32) * TOK_DEV)[:, None]
    chosen_by_expert = jnp.swapaxes(chosen, 0, 1)
    gates_by_expert = jnp.swapaxes(gates, 0, 1)

    def one_expert(total, inputs):
        gate_rows, up_rows, down_rows, pick_local, gate_values = inputs
        pick_rows = (slab_base + pick_local).reshape(-1).astype(jnp.int32)
        picked = jnp.take(tokens, pick_rows, axis=0)
        gate_part = jnp.dot(picked, gate_rows, preferred_element_type=jnp.float32)
        up_part = jnp.dot(picked, up_rows, preferred_element_type=jnp.float32)
        hidden = (jax.nn.silu(gate_part) * up_part).astype(jnp.bfloat16)
        expert_out = jnp.dot(hidden, down_rows, preferred_element_type=jnp.float32)
        weighted = gate_values.reshape(-1)[:, None] * expert_out
        return total.at[pick_rows].add(weighted), None

    start_total = jnp.zeros((tokens.shape[0], model_width), jnp.float32)
    total, unused = lax.scan(one_expert, start_total, (w_gate, w_up, w_down, chosen_by_expert, gates_by_expert))
    return total.astype(jnp.bfloat16)
```

```python
import jax
import jax.numpy as jnp
from jax import lax
from jax.experimental import pallas as pl
from jax.experimental.pallas import tpu as pltpu
from jax.sharding import PartitionSpec as P

MESH = pl.DeviceIdType.MESH
OFFSET = (0, 1, -1, 2, -2, 3, -3, 4)
PEERS = 16
CHUNKS = 4
SLOTS = 8


def moe_kernel(
    tok, cho, gat, wg, wu, wd, o,
    onehot, gcol, gmix, stage, xin, wgu, wdn, acc, hid, ost, ret,
    tok_send, tok_recv, ret_send, ret_recv,
    slot_recv, ring_send, sib_send, sib_recv, cross_send,
):
    dp, ex = lax.axis_index("dp"), lax.axis_index("expert")
    x_hi, z = dp // 8, dp % 8
    y, x_lo, c = ex // 4, (ex // 2) % 2, ex % 2
    x = x_hi * 2 + x_lo
    per = cho.shape[2]
    rows = PEERS * per
    wide = wg.shape[1]

    def device(xx, yy, zz, cc):
        xx, yy, zz = xx % 4, yy % 4, zz % 8
        return ((xx // 2) * 8 + zz, yy * 4 + (xx % 2) * 2 + cc)

    def shard_of(slot, p):
        column = c if p == 0 else 1 - c
        return column * 8 + (z + OFFSET[slot] + 8) % 8

    up, down = device(x, y, z + 1, c), device(x, y, z + 7, c)
    sibling = device(x, y, z, 1 - c)
    across = device(x + 2, y, z, 1 - c)
    native = c == x_hi

    barrier = pltpu.get_barrier_semaphore()

    def greet(r, carry):
        pl.semaphore_signal(
            barrier, inc=1, device_id=device(x + r % 4, y + r // 4, z, c), device_id_type=MESH
        )
        return carry

    lax.fori_loop(1, PEERS, greet, 0)
    for other in (up, down, sibling, across):
        pl.semaphore_signal(barrier, inc=1, device_id=other, device_id_type=MESH)

    def weight(k, slot, p):
        return wdn.at[slot, p] if k == 2 else wgu.at[k, slot, p]

    sources = (wg.at[0], wu.at[0], wd.at[0])

    @pl.when(native)
    def _():
        for k in range(3):
            pltpu.make_async_copy(sources[k], weight(k, 0, 0), slot_recv.at[k, 0]).start()

    eye = lax.broadcasted_iota(jnp.int32, (per, per), 0) == lax.broadcasted_iota(
        jnp.int32, (per, per), 1
    )
    token_id = lax.broadcasted_iota(jnp.int32, (per, onehot.shape[1]), 1).astype(jnp.float32)
    for r in range(PEERS):
        xx, yy = (x + r % 4) % 4, (y + r // 4) % 4
        e = yy * 4 + (xx % 2) * 2 + xx // 2
        picks = cho[0, pl.ds(e, 1), :].astype(jnp.float32)
        weights = gat[0, pl.ds(e, 1), :]
        pick_col = jnp.sum(jnp.where(eye, picks, 0.0), axis=1, keepdims=True)
        gate_col = jnp.sum(jnp.where(eye, weights, 0.0), axis=1, keepdims=True)
        hit = token_id == pick_col
        onehot[pl.ds(r * per, per), :] = jnp.where(hit, 1.0, 0.0).astype(jnp.bfloat16)
        gcol[pl.ds(r * per, per), :] = jnp.where(hit, gate_col, 0.0)

    pl.semaphore_wait(barrier, PEERS - 1 + 4)

    def cross(k):
        return pltpu.make_async_remote_copy(
            src_ref=sources[k], dst_ref=weight(k, 0, 0), send_sem=cross_send.at[k],
            recv_sem=slot_recv.at[k, 0], device_id=across, device_id_type=MESH,
        )

    @pl.when(jnp.logical_not(native))
    def _():
        for k in range(2):
            cross(k).start()

    def arrived(k, slot):
        pltpu.make_async_copy(
            weight(k, slot, 0), weight(k, slot, 0), slot_recv.at[k, slot]
        ).wait()

    def to_sibling(k, slot):
        return pltpu.make_async_remote_copy(
            src_ref=weight(k, slot, 0), dst_ref=weight(k, slot, 1), send_sem=sib_send.at[k, slot],
            recv_sem=sib_recv.at[k, slot], device_id=sibling, device_id_type=MESH,
        )

    def hop(k, src, dst, target):
        return pltpu.make_async_remote_copy(
            src_ref=weight(k, src, 0), dst_ref=weight(k, dst, 0), send_sem=ring_send.at[k, dst],
            recv_sem=slot_recv.at[k, dst], device_id=target, device_id_type=MESH,
        )

    def last_hop(k):
        return hop(k, 6 - c, 7, device(x, y, z + 1 + 6 * c, c))

    def spread(k, slot):
        if slot == 0:
            hop(k, 0, 2, up).start()
            hop(k, 0, 1, down).start()
        elif slot in (1, 3):
            hop(k, slot, slot + 2, down).start()
        elif slot in (2, 4):
            hop(k, slot, slot + 2, up).start()
        if slot == 5:

            @pl.when(c == 1)
            def _():
                last_hop(k).start()

        if slot == 6:

            @pl.when(c == 0)
            def _():
                last_hop(k).start()

        to_sibling(k, slot).start()

    @pl.when(native)
    def _():
        for k in range(2):
            arrived(k, 0)
            spread(k, 0)

    def send_tokens(g):
        for i in range(4):
            j = shard_of(2 * g + i // 2, i % 2)
            stage[g, :, pl.ds(i * 256, 256)] = jnp.dot(
                onehot[...],
                tok[:, pl.ds(pl.multiple_of(j * 256, 256), 256)],
                preferred_element_type=jnp.float32,
            ).astype(jnp.bfloat16)

        def send(r, carry):
            block = pl.ds(pl.multiple_of(r * per, per), per)
            pltpu.make_async_remote_copy(
                src_ref=stage.at[g, block], dst_ref=xin.at[g, block], send_sem=tok_send.at[g],
                recv_sem=tok_recv.at[g], device_id=device(x + r % 4, y + r // 4, z, c),
                device_id_type=MESH,
            ).start()
            return carry

        lax.fori_loop(1, PEERS, send, 0)
        xin[g, pl.ds(0, per), :] = stage[g, pl.ds(0, per), :]

    for g in range(CHUNKS):
        send_tokens(g)

    @pl.when(jnp.logical_not(native))
    def _():
        cross(2).start()
        for k in range(2):
            arrived(k, 0)
            spread(k, 0)

    mixed = gcol[...].T
    high = mixed.astype(jnp.bfloat16)
    gmix[0] = high
    gmix[1] = (mixed - high.astype(jnp.float32)).astype(jnp.bfloat16)

    def from_sibling(k, slot):
        pltpu.make_async_copy(
            weight(k, slot, 1), weight(k, slot, 1), sib_recv.at[k, slot]
        ).wait()

    others = pl.ds(per, rows - per)
    for g in range(CHUNKS):
        step_slots = (2 * g + 1, 2 * g + 2) if g < 3 else (7,)
        for slot in step_slots:
            for k in range(2):
                arrived(k, slot)
                spread(k, slot)
        if g == 2:
            arrived(2, 0)
            spread(2, 0)
        for slot in (2 * g, 2 * g + 1):
            for k in range(2):
                from_sibling(k, slot)
        pltpu.make_async_copy(xin.at[g, others], xin.at[g, others], tok_recv.at[g]).wait()

        def multiply(n, carry):
            k, tile = n // 3, n % 3
            part = wgu[k, pl.ds(2 * g, 2), :, :, pl.ds(pl.multiple_of(tile * 256, 256), 256)]
            product = jnp.dot(
                xin[g], part.reshape(4 * wide, 256), preferred_element_type=jnp.float32
            )
            if g == 0:
                acc[n] = product
            else:
                acc[n] += product
            return carry

        lax.fori_loop(0, 6, multiply, 0)

    for tile in range(3):
        gate_part = acc[tile]
        hid[:, pl.ds(tile * 256, 256)] = (
            gate_part / (1.0 + jnp.exp(-gate_part)) * acc[3 + tile]
        ).astype(jnp.bfloat16)

    for slot in range(SLOTS):
        if slot > 0:
            arrived(2, slot)
            spread(2, slot)
        from_sibling(2, slot)
        for p in range(2):
            ost[slot, :, pl.ds(p * 256, 256)] = jnp.dot(
                hid[...], wdn[slot, p], preferred_element_type=jnp.float32
            ).astype(jnp.bfloat16)

        def give_back(r, carry):
            block = pl.ds(pl.multiple_of(r * per, per), per)
            pltpu.make_async_remote_copy(
                src_ref=ost.at[slot, block], dst_ref=ret.at[slot, block],
                send_sem=ret_send.at[slot], recv_sem=ret_recv.at[slot],
                device_id=device(x + 4 - r % 4, y + 4 - r // 4, z, c), device_id_type=MESH,
            ).start()
            return carry

        lax.fori_loop(1, PEERS, give_back, 0)
        ret[slot, pl.ds(0, per), :] = ost[slot, pl.ds(0, per), :]

    for slot in range(SLOTS):
        pltpu.make_async_copy(
            ret.at[slot, others], ret.at[slot, others], ret_recv.at[slot]
        ).wait()
        for p in range(2):
            half = ret[slot, :, pl.ds(p * 256, 256)]
            j = shard_of(slot, p)
            o[:, pl.ds(pl.multiple_of(j * 256, 256), 256)] = (
                jnp.dot(gmix[0], half, preferred_element_type=jnp.float32)
                + jnp.dot(gmix[1], half, preferred_element_type=jnp.float32)
            ).astype(jnp.bfloat16)

    for g in range(CHUNKS):
        pltpu.make_async_copy(stage.at[g, others], stage.at[g, others], tok_send.at[g]).wait()
    for slot in range(SLOTS):
        pltpu.make_async_copy(ost.at[slot, others], ost.at[slot, others], ret_send.at[slot]).wait()
    for k in range(3):
        for slot in range(SLOTS):
            to_sibling(k, slot).wait_send()
            if 0 < slot < 7:
                hop(k, slot, slot, up).wait_send()
        last_hop(k).wait_send()

    @pl.when(jnp.logical_not(native))
    def _():
        for k in range(3):
            cross(k).wait_send()


def shards(tokens, chosen, gates, w_gate, w_up, w_down):
    count, width = tokens.shape
    per = chosen.shape[2]
    rows = PEERS * per
    depth, hidden = w_gate.shape[1:]
    vmem = pl.BlockSpec(memory_space=pltpu.VMEM)
    hbm = pl.BlockSpec(memory_space=pl.ANY)
    bf16, f32 = jnp.bfloat16, jnp.float32
    dma = pltpu.SemaphoreType.DMA
    return pl.pallas_call(
        moe_kernel,
        out_shape=jax.ShapeDtypeStruct((count, width), bf16),
        in_specs=[vmem, vmem, vmem, hbm, hbm, hbm],
        out_specs=vmem,
        scratch_shapes=[
            pltpu.VMEM((rows, count), bf16),
            pltpu.VMEM((rows, count), f32),
            pltpu.VMEM((2, count, rows), bf16),
            pltpu.VMEM((CHUNKS, rows, width // CHUNKS), bf16),
            pltpu.VMEM((CHUNKS, rows, width // CHUNKS), bf16),
            pltpu.VMEM((2, SLOTS, 2, depth, hidden), bf16),
            pltpu.VMEM((SLOTS, 2, hidden, depth), bf16),
            pltpu.VMEM((6, rows, hidden // 3), f32),
            pltpu.VMEM((rows, hidden), bf16),
            pltpu.VMEM((SLOTS, rows, width // SLOTS), bf16),
            pltpu.VMEM((SLOTS, rows, width // SLOTS), bf16),
            dma((CHUNKS,)),
            dma((CHUNKS,)),
            dma((SLOTS,)),
            dma((SLOTS,)),
            dma((3, SLOTS)),
            dma((3, SLOTS)),
            dma((3, SLOTS)),
            dma((3, SLOTS)),
            dma((3,)),
        ],
        compiler_params=pltpu.CompilerParams(
            collective_id=0, has_side_effects=True, vmem_limit_bytes=60 * 2**20
        ),
        cost_estimate=pl.CostEstimate(
            flops=11 * 10**9, bytes_accessed=8 * 2**20, transcendentals=rows * hidden
        ),
        name="moe",
    )(tokens, chosen, gates, w_gate, w_up, w_down)


def solution(mesh):
    in_specs = (
        P(("dp", "expert"), None),
        P(("dp", "expert"), None, None),
        P(("dp", "expert"), None, None),
        P("expert", "dp", None),
        P("expert", "dp", None),
        P("expert", None, "dp"),
    )
    out_specs = P(("dp", "expert"), None)
    return jax.shard_map(shards, mesh=mesh, in_specs=in_specs, out_specs=out_specs, check_vma=False)
```

```python
import jax
import jax.numpy as jnp
from jax import lax
from jax.experimental import pallas as pl
from jax.experimental.pallas import tpu as pltpu
from jax.sharding import PartitionSpec as P

MESH = pl.DeviceIdType.MESH
OFFSET = (0, 1, -1, 2, -2, 3, -3, 4)
PEERS = 16
SLOTS = 8
HALVES = 2
GROUPS = ((0,), (1, 2), (3, 4), (5, 6), (7,))


def moe_kernel(
    tok_hbm, cho, gat, wg, wu, wd, o,
    tok, onehot, gcol, gmix, stage, xin, wgu, wdn, acc, hid, ost, ret,
    tok_sem, tok_send, tok_recv, ret_send, ret_recv,
    own_recv, own_send, pair_recv, pair_send, down_recv, down_send, swap_recv, swap_send, first_send, far_send,
):
    dp, ex = lax.axis_index("dp"), lax.axis_index("expert")
    x_hi, z = dp // 8, dp % 8
    y, x_lo, c = ex // 4, (ex // 2) % 2, ex % 2
    x = x_hi * 2 + x_lo
    per = cho.shape[2]
    rows = PEERS * per
    depth, hidden = wg.shape[1:]
    tiles = hidden // 256
    wide = 2 * depth

    def device(xx, yy, zz, cc):
        xx, yy, zz = xx % 4, yy % 4, zz % 8
        return ((xx // 2) * 8 + zz, yy * 4 + (xx % 2) * 2 + cc)

    def shard_columns(slot, q):
        j = q * 8 + (z + OFFSET[slot] + 8) % 8
        return pl.ds(pl.multiple_of(j * depth, depth), depth)

    def remote(src, dst, send, recv, target):
        return pltpu.make_async_remote_copy(
            src_ref=src, dst_ref=dst, send_sem=send, recv_sem=recv, device_id=target,
            device_id_type=MESH,
        )

    up, down = device(x, y, z + 1, c), device(x, y, z + 7, c)
    sibling = device(x, y, z, 1 - c)
    native = c == x_hi

    barrier = pltpu.get_barrier_semaphore()

    def greet(r, carry):
        pl.semaphore_signal(
            barrier, inc=1, device_id=device(x + r % 4, y + r // 4, z, c), device_id_type=MESH
        )
        return carry

    greeted = [(x, y, z + dz, cc) for dz in (1, 7) for cc in range(2)]
    greeted += [(x, y, z, 1 - c), (x + 2, y, z, 1 - c)]
    for other in [device(*there) for there in greeted]:
        pl.semaphore_signal(barrier, inc=1, device_id=other, device_id_type=MESH)
    lax.fori_loop(1, PEERS, greet, 0)

    fetch = pltpu.make_async_copy(tok_hbm, tok, tok_sem.at[0])
    fetch.start()

    near, far = x_hi, 1 - x_hi
    sources = (wg.at[0], wu.at[0])
    half = depth // HALVES

    def rows_of(h):
        return pl.ds(h * half, half)

    for k in range(2):
        for h in range(HALVES):
            start = pltpu.make_async_copy
            part = sources[k].at[rows_of(h)], wgu.at[k, 0, near, rows_of(h)]

            @pl.when(native & (c == k))
            def _():
                start(*part, own_recv.at[near, 0, h]).start()

            @pl.when(native & (c != k))
            def _():
                start(*part, pair_recv.at[near, 0, h]).start()

    @pl.when(native)
    def _():
        pltpu.make_async_copy(wd.at[0], wdn.at[0, c], down_recv.at[0]).start()

    eye = lax.broadcasted_iota(jnp.int32, (per, per), 0) == lax.broadcasted_iota(
        jnp.int32, (per, per), 1
    )
    token_id = lax.broadcasted_iota(jnp.int32, (per, onehot.shape[1]), 1).astype(jnp.float32)
    for r in range(PEERS):
        xx, yy = (x + r % 4) % 4, (y + r // 4) % 4
        e = yy * 4 + (xx % 2) * 2 + xx // 2
        picks = cho[0, pl.ds(e, 1), :].astype(jnp.float32)
        weights = gat[0, pl.ds(e, 1), :]
        pick_col = jnp.sum(jnp.where(eye, picks, 0.0), axis=1, keepdims=True)
        gate_col = jnp.sum(jnp.where(eye, weights, 0.0), axis=1, keepdims=True)
        hit = token_id == pick_col
        onehot[pl.ds(r * per, per), :] = jnp.where(hit, 1.0, 0.0).astype(jnp.bfloat16)
        gcol[pl.ds(r * per, per), :] = jnp.where(hit, gate_col, 0.0)

    pl.semaphore_wait(barrier, PEERS - 1 + len(greeted))

    def near_first(k, h, there):
        slot, index = (2, 0) if there == 1 else (1, 1)
        return remote(
            sources[k].at[rows_of(h)], wgu.at[k, slot, near, rows_of(h)],
            first_send.at[index, k, h], own_recv.at[near, slot, h], device(x, y, z + there, k),
        )

    def near_sibling(k, h, semaphores):
        return remote(
            sources[k].at[rows_of(h)], wgu.at[k, 0, near, rows_of(h)],
            first_send.at[2, k, h], semaphores.at[near, 0, h], sibling,
        )

    def far_first(k, h):
        return remote(
            sources[k].at[rows_of(h)], wgu.at[k, 0, x_hi, rows_of(h)],
            first_send.at[0, k, h], own_recv.at[x_hi, 0, h], device(x + 2, y, z, k),
        )

    def near_firsts(act):
        for h in range(HALVES):
            for k in range(2):
                act(near_first(k, h, 1))
                act(near_first(k, h, 7))
        for h in range(HALVES):
            for k in range(2):

                @pl.when(c == k)
                def _():
                    act(near_sibling(k, h, pair_recv))

                @pl.when(c != k)
                def _():
                    act(near_sibling(k, h, own_recv))

    def far_firsts(act):
        for h in range(HALVES):
            for k in range(2):
                act(far_first(k, h))

    def far_down():
        return remote(
            wd.at[0], wdn.at[0, 1 - c], far_send.at[0], down_recv.at[0],
            device(x + 2, y, z, 1 - c),
        )

    @pl.when(native)
    def _():
        near_firsts(lambda copy: copy.start())

    @pl.when(jnp.logical_not(native))
    def _():
        far_firsts(lambda copy: copy.start())

    def arrived(slot, q, h):
        part = wgu.at[c, slot, q, rows_of(h)]
        pltpu.make_async_copy(part, part, own_recv.at[q, slot, h]).wait()

    def pair(slot, q, h):
        part = wgu.at[c, slot, q, rows_of(h)]
        return remote(part, part, pair_send.at[q, slot, h], pair_recv.at[q, slot, h], sibling)

    def from_pair(slot, q, h):
        part = wgu.at[1 - c, slot, q, rows_of(h)]
        pltpu.make_async_copy(part, part, pair_recv.at[q, slot, h]).wait()

    def hop(src, dst, q, h, target):
        return remote(
            wgu.at[c, src, q, rows_of(h)], wgu.at[c, dst, q, rows_of(h)], own_send.at[q, dst, h],
            own_recv.at[q, dst, h], target,
        )

    def down_arrived(slot):
        part = wdn.at[slot, c]
        pltpu.make_async_copy(part, part, down_recv.at[slot]).wait()

    def swap(slot):
        part = wdn.at[slot, c]
        return remote(part, part, swap_send.at[slot], swap_recv.at[slot], sibling)

    def from_swap(slot):
        part = wdn.at[slot, 1 - c]
        pltpu.make_async_copy(part, part, swap_recv.at[slot]).wait()

    def down_hop(src, dst, target):
        return remote(
            wdn.at[src, c], wdn.at[dst, c], down_send.at[dst], down_recv.at[dst], target
        )

    last_src, last_target = 6 - c, device(x, y, z + 1 + 6 * c, c)

    def onward(slot, send):
        if slot == 0:
            send(0, 2, up)
            send(0, 1, down)
        elif slot in (1, 3):
            send(slot, slot + 2, down)
        elif slot in (2, 4):
            send(slot, slot + 2, up)
        elif slot in (5, 6):

            @pl.when(last_src == slot)
            def _():
                send(slot, 7, last_target)

    def spread(slot, q, h):
        arrived(slot, q, h)
        onward(slot, lambda src, dst, target: hop(src, dst, q, h, target).start())
        pair(slot, q, h).start()

    def columns(group):
        return pl.ds(group[0] * wide, len(group) * wide)

    def token_block(ref, group, r):
        return ref.at[pl.ds(pl.multiple_of(r * per, per), per), columns(group)]

    def send_tokens(g):
        group = GROUPS[g]
        for slot in group:
            for q in range(2):
                stage[:, pl.ds(slot * wide + q * depth, depth)] = jnp.dot(
                    onehot[...], tok[:, shard_columns(slot, q)], preferred_element_type=jnp.float32
                ).astype(jnp.bfloat16)

        def send(r, carry):
            remote(
                token_block(stage, group, r), token_block(xin, group, r), tok_send.at[g],
                tok_recv.at[g], device(x + r % 4, y + r // 4, z, c),
            ).start()
            return carry

        lax.fori_loop(1, PEERS, send, 0)
        xin[pl.ds(0, per), columns(group)] = stage[pl.ds(0, per), columns(group)]

    def spread_group(g, q, h):
        for slot in GROUPS[g]:
            spread(slot, q, h)

    fetch.wait()
    send_tokens(0)
    spread_group(0, far, 0)
    spread_group(1, near, 0)
    send_tokens(1)
    spread_group(0, far, 1)
    spread_group(1, near, 1)
    for g in range(2, len(GROUPS)):
        send_tokens(g)

    @pl.when(jnp.logical_not(native))
    def _():
        far_down().start()

    mixed = gcol[...].T
    high = mixed.astype(jnp.bfloat16)
    gmix[0] = high
    gmix[1] = (mixed - high.astype(jnp.float32)).astype(jnp.bfloat16)

    others = pl.ds(per, rows - per)

    def add_products(g):
        group = GROUPS[g]
        for q in (near, far):
            for slot in group:
                for h in range(HALVES):
                    from_pair(slot, q, h)
        if g == 0:
            for h in range(HALVES):
                arrived(0, near, h)
        block = xin.at[others, columns(group)]
        pltpu.make_async_copy(block, block, tok_recv.at[g]).wait()

        def multiply(n, carry):
            k, tile = n // tiles, n % tiles
            part = wgu[
                k, pl.ds(group[0], len(group)), :, :, pl.ds(pl.multiple_of(tile * 256, 256), 256)
            ]
            product = jnp.dot(
                xin[:, columns(group)], part.reshape(len(group) * wide, 256),
                preferred_element_type=jnp.float32,
            )
            if g == 0:
                acc[n] = product
            else:
                acc[n] += product
            return carry

        lax.fori_loop(0, 2 * tiles, multiply, 0)

    for g in range(2, len(GROUPS)):
        for h in range(HALVES):
            spread_group(g - 1, far, h)
            spread_group(g, near, h)
        add_products(g - 2)
        if g == 3:
            down_arrived(0)
            swap(0).start()
    add_products(3)
    for h in range(HALVES):
        spread_group(4, far, h)
    onward(0, lambda src, dst, target: down_hop(src, dst, target).start())
    add_products(4)

    for tile in range(tiles):
        gate_part = acc[tile]
        hid[:, pl.ds(tile * 256, 256)] = (
            gate_part / (1.0 + jnp.exp(-gate_part)) * acc[tiles + tile]
        ).astype(jnp.bfloat16)

    for slot in range(SLOTS):
        if slot > 0:
            down_arrived(slot)
            onward(slot, lambda src, dst, target: down_hop(src, dst, target).start())
            swap(slot).start()
        from_swap(slot)
        for q in range(2):
            ost[slot, :, pl.ds(q * depth, depth)] = jnp.dot(
                hid[...], wdn[slot, q], preferred_element_type=jnp.float32
            ).astype(jnp.bfloat16)

        def give_back(r, carry):
            block = pl.ds(pl.multiple_of(r * per, per), per)
            remote(
                ost.at[slot, block], ret.at[slot, block], ret_send.at[slot], ret_recv.at[slot],
                device(x + 4 - r % 4, y + 4 - r // 4, z, c),
            ).start()
            return carry

        lax.fori_loop(1, PEERS, give_back, 0)
        ret[slot, pl.ds(0, per), :] = ost[slot, pl.ds(0, per), :]

    for slot in range(SLOTS):
        block = ret.at[slot, others]
        pltpu.make_async_copy(block, block, ret_recv.at[slot]).wait()
        for q in range(2):
            part = ret[slot, :, pl.ds(q * depth, depth)]
            o[:, shard_columns(slot, q)] = (
                jnp.dot(gmix[0], part, preferred_element_type=jnp.float32)
                + jnp.dot(gmix[1], part, preferred_element_type=jnp.float32)
            ).astype(jnp.bfloat16)

    for g, group in enumerate(GROUPS):
        block = stage.at[others, columns(group)]
        pltpu.make_async_copy(block, block, tok_send.at[g]).wait()
    for slot in range(SLOTS):
        block = ost.at[slot, others]
        pltpu.make_async_copy(block, block, ret_send.at[slot]).wait()
        swap(slot).wait_send()
        for h in range(HALVES):
            for q in (near, far):
                if slot > 0 or q is far:
                    pair(slot, q, h).wait_send()
                if slot > 2 or (slot > 0 and q is far):
                    hop(0, slot, q, h, up).wait_send()
        if slot > 0:
            down_hop(0, slot, up).wait_send()
    @pl.when(native)
    def _():
        near_firsts(lambda copy: copy.wait_send())

    @pl.when(jnp.logical_not(native))
    def _():
        far_firsts(lambda copy: copy.wait_send())
        far_down().wait_send()


def shards(tokens, chosen, gates, w_gate, w_up, w_down):
    count, width = tokens.shape
    per = chosen.shape[2]
    rows = PEERS * per
    depth, hidden = w_gate.shape[1:]
    vmem = pl.BlockSpec(memory_space=pltpu.VMEM)
    hbm = pl.BlockSpec(memory_space=pl.ANY)
    bf16, f32 = jnp.bfloat16, jnp.float32
    dma = pltpu.SemaphoreType.DMA
    return pl.pallas_call(
        moe_kernel,
        out_shape=pltpu.VMEM((count, width), bf16),
        in_specs=[hbm, vmem, vmem, hbm, hbm, hbm],
        out_specs=vmem,
        scratch_shapes=[
            pltpu.VMEM((count, width), bf16),
            pltpu.VMEM((rows, count), bf16),
            pltpu.VMEM((rows, count), f32),
            pltpu.VMEM((2, count, rows), bf16),
            pltpu.VMEM((rows, width), bf16),
            pltpu.VMEM((rows, width), bf16),
            pltpu.VMEM((2, SLOTS, 2, depth, hidden), bf16),
            pltpu.VMEM((SLOTS, 2, hidden, depth), bf16),
            pltpu.VMEM((2 * hidden // 256, rows, 256), f32),
            pltpu.VMEM((rows, hidden), bf16),
            pltpu.VMEM((SLOTS, rows, width // SLOTS), bf16),
            pltpu.VMEM((SLOTS, rows, width // SLOTS), bf16),
            dma((1,)),
            dma((len(GROUPS),)),
            dma((len(GROUPS),)),
            dma((SLOTS,)),
            dma((SLOTS,)),
            dma((2, SLOTS, HALVES)),
            dma((2, SLOTS, HALVES)),
            dma((2, SLOTS, HALVES)),
            dma((2, SLOTS, HALVES)),
            dma((SLOTS,)),
            dma((SLOTS,)),
            dma((SLOTS,)),
            dma((SLOTS,)),
            dma((3, 2, HALVES)),
            dma((1,)),
        ],
        compiler_params=pltpu.CompilerParams(
            collective_id=0, has_side_effects=True, vmem_limit_bytes=61 * 2**20
        ),
        cost_estimate=pl.CostEstimate(
            flops=11 * 10**9, bytes_accessed=8 * 2**20, transcendentals=rows * hidden
        ),
        name="moe",
    )(tokens, chosen, gates, w_gate, w_up, w_down)


def solution(mesh):
    in_specs = (
        P(("dp", "expert"), None),
        P(("dp", "expert"), None, None),
        P(("dp", "expert"), None, None),
        P("expert", "dp", None),
        P("expert", "dp", None),
        P("expert", None, "dp"),
    )
    out_specs = P(("dp", "expert"), None)
    return jax.shard_map(shards, mesh=mesh, in_specs=in_specs, out_specs=out_specs, check_vma=False)
```

```python
import jax
import jax.numpy as jnp
from jax import lax
from jax.experimental import pallas as pl
from jax.experimental.pallas import tpu as pltpu
from jax.sharding import PartitionSpec as P

MESH = pl.DeviceIdType.MESH
OFFSET = (0, 1, -1, 2, -2, 3, -3, 4)
PEERS = 16
SLOTS = 8
HALVES = 2
GROUPS = ((0,), (1, 2), (3, 4), (5, 6), (7,))


def moe_kernel(
    tok_hbm, cho, gat, wg, wu, wd, o,
    tok, onehot, gcol, gmix, stage, xin, wgu, wdn, acc, hid, ost, ret,
    tok_sem, tok_send, tok_recv, ret_send, ret_recv,
    own_recv, own_send, pair_recv, pair_send, down_recv, down_send, swap_recv, swap_send, first_send, far_send,
):
    dp, ex = lax.axis_index("dp"), lax.axis_index("expert")
    x_hi, z = dp // 8, dp % 8
    y, x_lo, c = ex // 4, (ex // 2) % 2, ex % 2
    x = x_hi * 2 + x_lo
    per = cho.shape[2]
    rows = PEERS * per
    depth, hidden = wg.shape[1:]
    tiles = hidden // 256
    wide = 2 * depth

    def device(xx, yy, zz, cc):
        xx, yy, zz = xx % 4, yy % 4, zz % 8
        return ((xx // 2) * 8 + zz, yy * 4 + (xx % 2) * 2 + cc)

    def shard_columns(slot, q):
        j = q * 8 + (z + OFFSET[slot] + 8) % 8
        return pl.ds(pl.multiple_of(j * depth, depth), depth)

    def remote(src, dst, send, recv, target):
        return pltpu.make_async_remote_copy(
            src_ref=src, dst_ref=dst, send_sem=send, recv_sem=recv, device_id=target,
            device_id_type=MESH,
        )

    up, down = device(x, y, z + 1, c), device(x, y, z + 7, c)
    sibling = device(x, y, z, 1 - c)
    native = c == x_hi

    barrier = pltpu.get_barrier_semaphore()

    def greet(r, carry):
        pl.semaphore_signal(
            barrier, inc=1, device_id=device(x + r % 4, y + r // 4, z, c), device_id_type=MESH
        )
        return carry

    greeted = [(x, y, z + dz, cc) for dz in (1, 7) for cc in range(2)]
    greeted += [(x, y, z, 1 - c), (x + 2, y, z, 1 - c)]
    for other in [device(*there) for there in greeted]:
        pl.semaphore_signal(barrier, inc=1, device_id=other, device_id_type=MESH)
    lax.fori_loop(1, PEERS, greet, 0)

    fetch = pltpu.make_async_copy(tok_hbm, tok, tok_sem.at[0])
    fetch.start()

    near, far = x_hi, 1 - x_hi
    sources = (wg.at[0], wu.at[0])
    half = depth // HALVES

    def rows_of(h):
        return pl.ds(h * half, half)

    for k in range(2):
        for h in range(HALVES):
            start = pltpu.make_async_copy
            part = sources[k].at[rows_of(h)], wgu.at[k, 0, near, rows_of(h)]

            @pl.when(native & (c == k))
            def _():
                start(*part, own_recv.at[near, 0, h]).start()

            @pl.when(native & (c != k))
            def _():
                start(*part, pair_recv.at[near, 0, h]).start()

    @pl.when(native)
    def _():
        pltpu.make_async_copy(wd.at[0], wdn.at[0, c], down_recv.at[0]).start()

    eye = lax.broadcasted_iota(jnp.int32, (per, per), 0) == lax.broadcasted_iota(
        jnp.int32, (per, per), 1
    )
    token_id = lax.broadcasted_iota(jnp.int32, (per, onehot.shape[1]), 1).astype(jnp.float32)
    for r in range(PEERS):
        xx, yy = (x + r % 4) % 4, (y + r // 4) % 4
        e = yy * 4 + (xx % 2) * 2 + xx // 2
        picks = cho[0, pl.ds(e, 1), :].astype(jnp.float32)
        weights = gat[0, pl.ds(e, 1), :]
        pick_col = jnp.sum(jnp.where(eye, picks, 0.0), axis=1, keepdims=True)
        gate_col = jnp.sum(jnp.where(eye, weights, 0.0), axis=1, keepdims=True)
        hit = token_id == pick_col
        onehot[pl.ds(r * per, per), :] = jnp.where(hit, 1.0, 0.0).astype(jnp.bfloat16)
        gcol[pl.ds(r * per, per), :] = jnp.where(hit, gate_col, 0.0)

    pl.semaphore_wait(barrier, PEERS - 1 + len(greeted))

    def near_first(k, h, there):
        slot, index = (2, 0) if there == 1 else (1, 1)
        return remote(
            sources[k].at[rows_of(h)], wgu.at[k, slot, near, rows_of(h)],
            first_send.at[index, k, h], own_recv.at[near, slot, h], device(x, y, z + there, k),
        )

    def near_sibling(k, h, semaphores):
        return remote(
            sources[k].at[rows_of(h)], wgu.at[k, 0, near, rows_of(h)],
            first_send.at[2, k, h], semaphores.at[near, 0, h], sibling,
        )

    def far_first(k, h):
        return remote(
            sources[k].at[rows_of(h)], wgu.at[k, 0, x_hi, rows_of(h)],
            first_send.at[0, k, h], own_recv.at[x_hi, 0, h], device(x + 2, y, z, k),
        )

    def near_firsts(act):
        for h in range(HALVES):
            for k in range(2):
                act(near_first(k, h, 1))
                act(near_first(k, h, 7))
        for h in range(HALVES):
            for k in range(2):

                @pl.when(c == k)
                def _():
                    act(near_sibling(k, h, pair_recv))

                @pl.when(c != k)
                def _():
                    act(near_sibling(k, h, own_recv))

    def far_firsts(act):
        for h in range(HALVES):
            for k in range(2):
                act(far_first(k, h))

    def far_down():
        return remote(
            wd.at[0], wdn.at[0, 1 - c], far_send.at[0], down_recv.at[0],
            device(x + 2, y, z, 1 - c),
        )

    @pl.when(native)
    def _():
        near_firsts(lambda copy: copy.start())

    @pl.when(jnp.logical_not(native))
    def _():
        far_firsts(lambda copy: copy.start())

    def arrived(slot, q, h):
        part = wgu.at[c, slot, q, rows_of(h)]
        pltpu.make_async_copy(part, part, own_recv.at[q, slot, h]).wait()

    def pair(slot, q, h):
        part = wgu.at[c, slot, q, rows_of(h)]
        return remote(part, part, pair_send.at[q, slot, h], pair_recv.at[q, slot, h], sibling)

    def from_pair(slot, q, h):
        part = wgu.at[1 - c, slot, q, rows_of(h)]
        pltpu.make_async_copy(part, part, pair_recv.at[q, slot, h]).wait()

    def hop(src, dst, q, h, target):
        return remote(
            wgu.at[c, src, q, rows_of(h)], wgu.at[c, dst, q, rows_of(h)], own_send.at[q, dst, h],
            own_recv.at[q, dst, h], target,
        )

    def down_arrived(slot):
        part = wdn.at[slot, c]
        pltpu.make_async_copy(part, part, down_recv.at[slot]).wait()

    def swap(slot):
        part = wdn.at[slot, c]
        return remote(part, part, swap_send.at[slot], swap_recv.at[slot], sibling)

    def from_swap(slot):
        part = wdn.at[slot, 1 - c]
        pltpu.make_async_copy(part, part, swap_recv.at[slot]).wait()

    def down_hop(src, dst, target):
        return remote(
            wdn.at[src, c], wdn.at[dst, c], down_send.at[dst], down_recv.at[dst], target
        )

    last_src, last_target = 6 - c, device(x, y, z + 1 + 6 * c, c)

    def onward(slot, send):
        if slot == 0:
            send(0, 2, up)
            send(0, 1, down)
        elif slot in (1, 3):
            send(slot, slot + 2, down)
        elif slot in (2, 4):
            send(slot, slot + 2, up)
        elif slot in (5, 6):

            @pl.when(last_src == slot)
            def _():
                send(slot, 7, last_target)

    def spread(slot, q, h):
        arrived(slot, q, h)
        onward(slot, lambda src, dst, target: hop(src, dst, q, h, target).start())
        pair(slot, q, h).start()

    def columns(group):
        return pl.ds(group[0] * wide, len(group) * wide)

    def token_block(ref, group, r):
        return ref.at[pl.ds(pl.multiple_of(r * per, per), per), columns(group)]

    def send_tokens(g):
        group = GROUPS[g]
        for slot in group:
            for q in range(2):
                stage[:, pl.ds(slot * wide + q * depth, depth)] = jnp.dot(
                    onehot[...], tok[:, shard_columns(slot, q)], preferred_element_type=jnp.float32
                ).astype(jnp.bfloat16)

        def send(r, carry):
            remote(
                token_block(stage, group, r), token_block(xin, group, r), tok_send.at[g],
                tok_recv.at[g], device(x + r % 4, y + r // 4, z, c),
            ).start()
            return carry

        lax.fori_loop(1, PEERS, send, 0)
        xin[pl.ds(0, per), columns(group)] = stage[pl.ds(0, per), columns(group)]

    def spread_group(g, q, h):
        for slot in GROUPS[g]:
            spread(slot, q, h)

    fetch.wait()
    send_tokens(0)
    spread_group(0, far, 0)
    spread_group(1, near, 0)
    send_tokens(1)
    spread_group(0, far, 1)
    spread_group(1, near, 1)
    for g in range(2, len(GROUPS)):
        send_tokens(g)

    @pl.when(jnp.logical_not(native))
    def _():
        far_down().start()

    mixed = gcol[...].T
    high = mixed.astype(jnp.bfloat16)
    gmix[0] = high
    gmix[1] = (mixed - high.astype(jnp.float32)).astype(jnp.bfloat16)

    others = pl.ds(per, rows - per)

    def products_ready(g):
        group = GROUPS[g]
        for q in (near, far):
            for slot in group:
                for h in range(HALVES):
                    from_pair(slot, q, h)
        if g == 0:
            for h in range(HALVES):
                arrived(0, near, h)
        block = xin.at[others, columns(group)]
        pltpu.make_async_copy(block, block, tok_recv.at[g]).wait()

    def product(g, k, lanes):
        group = GROUPS[g]
        part = wgu[k, pl.ds(group[0], len(group)), :, :, lanes]
        return jnp.dot(
            xin[:, columns(group)], part.reshape(len(group) * wide, 256),
            preferred_element_type=jnp.float32,
        )

    def add_products(g):
        products_ready(g)

        def multiply(n, carry):
            k, tile = n // tiles, n % tiles
            more = product(g, k, pl.ds(pl.multiple_of(tile * 256, 256), 256))
            if g == 0:
                acc[n] = more
            else:
                acc[n] += more
            return carry

        lax.fori_loop(0, 2 * tiles, multiply, 0)

    def make_hidden(g):
        products_ready(g)
        for tile in range(tiles):
            lanes = pl.ds(tile * 256, 256)
            gate_part = acc[tile] + product(g, 0, lanes)
            up_part = acc[tiles + tile] + product(g, 1, lanes)
            hid[:, lanes] = (gate_part / (1.0 + jnp.exp(-gate_part)) * up_part).astype(jnp.bfloat16)

    for g in range(2, len(GROUPS)):
        for h in range(HALVES):
            spread_group(g - 1, far, h)
            spread_group(g, near, h)
        add_products(g - 2)
    add_products(3)
    for h in range(HALVES):
        spread_group(4, far, h)
    down_arrived(0)
    onward(0, lambda src, dst, target: down_hop(src, dst, target).start())
    swap(0).start()
    make_hidden(4)

    for slot in range(SLOTS):
        for fresh in next((g for g in GROUPS[1:] if g[0] == slot), ()):
            down_arrived(fresh)
            onward(fresh, lambda src, dst, target: down_hop(src, dst, target).start())
            swap(fresh).start()
        from_swap(slot)
        for q in range(2):
            ost[slot, :, pl.ds(q * depth, depth)] = jnp.dot(
                hid[...], wdn[slot, q], preferred_element_type=jnp.float32
            ).astype(jnp.bfloat16)

        def give_back(r, carry):
            block = pl.ds(pl.multiple_of(r * per, per), per)
            remote(
                ost.at[slot, block], ret.at[slot, block], ret_send.at[slot], ret_recv.at[slot],
                device(x + 4 - r % 4, y + 4 - r // 4, z, c),
            ).start()
            return carry

        lax.fori_loop(1, PEERS, give_back, 0)
        ret[slot, pl.ds(0, per), :] = ost[slot, pl.ds(0, per), :]

    for slot in range(SLOTS):
        block = ret.at[slot, others]
        pltpu.make_async_copy(block, block, ret_recv.at[slot]).wait()
        for q in range(2):
            part = ret[slot, :, pl.ds(q * depth, depth)]
            o[:, shard_columns(slot, q)] = (
                jnp.dot(gmix[0], part, preferred_element_type=jnp.float32)
                + jnp.dot(gmix[1], part, preferred_element_type=jnp.float32)
            ).astype(jnp.bfloat16)

    for g, group in enumerate(GROUPS):
        block = stage.at[others, columns(group)]
        pltpu.make_async_copy(block, block, tok_send.at[g]).wait()
    for slot in range(SLOTS):
        block = ost.at[slot, others]
        pltpu.make_async_copy(block, block, ret_send.at[slot]).wait()
        swap(slot).wait_send()
        for h in range(HALVES):
            for q in (near, far):
                if slot > 0 or q is far:
                    pair(slot, q, h).wait_send()
                if slot > 2 or (slot > 0 and q is far):
                    hop(0, slot, q, h, up).wait_send()
        if slot > 0:
            down_hop(0, slot, up).wait_send()
    @pl.when(native)
    def _():
        near_firsts(lambda copy: copy.wait_send())

    @pl.when(jnp.logical_not(native))
    def _():
        far_firsts(lambda copy: copy.wait_send())
        far_down().wait_send()


def shards(tokens, chosen, gates, w_gate, w_up, w_down):
    count, width = tokens.shape
    per = chosen.shape[2]
    rows = PEERS * per
    depth, hidden = w_gate.shape[1:]
    vmem = pl.BlockSpec(memory_space=pltpu.VMEM)
    hbm = pl.BlockSpec(memory_space=pl.ANY)
    bf16, f32 = jnp.bfloat16, jnp.float32
    dma = pltpu.SemaphoreType.DMA
    return pl.pallas_call(
        moe_kernel,
        out_shape=pltpu.VMEM((count, width), bf16),
        in_specs=[hbm, vmem, vmem, hbm, hbm, hbm],
        out_specs=vmem,
        scratch_shapes=[
            pltpu.VMEM((count, width), bf16),
            pltpu.VMEM((rows, count), bf16),
            pltpu.VMEM((rows, count), f32),
            pltpu.VMEM((2, count, rows), bf16),
            pltpu.VMEM((rows, width), bf16),
            pltpu.VMEM((rows, width), bf16),
            pltpu.VMEM((2, SLOTS, 2, depth, hidden), bf16),
            pltpu.VMEM((SLOTS, 2, hidden, depth), bf16),
            pltpu.VMEM((2 * hidden // 256, rows, 256), f32),
            pltpu.VMEM((rows, hidden), bf16),
            pltpu.VMEM((SLOTS, rows, width // SLOTS), bf16),
            pltpu.VMEM((SLOTS, rows, width // SLOTS), bf16),
            dma((1,)),
            dma((len(GROUPS),)),
            dma((len(GROUPS),)),
            dma((SLOTS,)),
            dma((SLOTS,)),
            dma((2, SLOTS, HALVES)),
            dma((2, SLOTS, HALVES)),
            dma((2, SLOTS, HALVES)),
            dma((2, SLOTS, HALVES)),
            dma((SLOTS,)),
            dma((SLOTS,)),
            dma((SLOTS,)),
            dma((SLOTS,)),
            dma((3, 2, HALVES)),
            dma((1,)),
        ],
        compiler_params=pltpu.CompilerParams(
            collective_id=0, has_side_effects=True, vmem_limit_bytes=61 * 2**20
        ),
        cost_estimate=pl.CostEstimate(
            flops=11 * 10**9, bytes_accessed=8 * 2**20, transcendentals=rows * hidden
        ),
        name="moe",
    )(tokens, chosen, gates, w_gate, w_up, w_down)


def solution(mesh):
    in_specs = (
        P(("dp", "expert"), None),
        P(("dp", "expert"), None, None),
        P(("dp", "expert"), None, None),
        P("expert", "dp", None),
        P("expert", "dp", None),
        P("expert", None, "dp"),
    )
    out_specs = P(("dp", "expert"), None)
    return jax.shard_map(shards, mesh=mesh, in_specs=in_specs, out_specs=out_specs, check_vma=False)
```

```python
import jax
import jax.numpy as jnp
from jax import lax
from jax.experimental import pallas as pl
from jax.experimental.pallas import tpu as pltpu
from jax.sharding import PartitionSpec as P

MESH = pl.DeviceIdType.MESH
OFFSET = (0, 1, -1, 2, -2, 3, -3, 4)
PEERS = 16
SLOTS = 8
HALVES = 2
GROUPS = ((0,), (1, 2), (3, 4), (5, 6), (7,))


def moe_kernel(
    tok_hbm, cho, gat, wg, wu, wd, o,
    tok, onehot, gcol, gmix, stage, xin, wgu, wdn, acc, hid, ost, ret,
    tok_sem, tok_send, tok_recv, ret_send, ret_recv,
    own_recv, own_send, pair_recv, pair_send, down_recv, down_send, swap_recv, swap_send, first_send, far_send,
):
    dp, ex = lax.axis_index("dp"), lax.axis_index("expert")
    x_hi, z = dp // 8, dp % 8
    y, x_lo, c = ex // 4, (ex // 2) % 2, ex % 2
    x = x_hi * 2 + x_lo
    per = cho.shape[2]
    rows = PEERS * per
    depth, hidden = wg.shape[1:]
    tiles = hidden // 256
    wide = 2 * depth

    def device(xx, yy, zz, cc):
        xx, yy, zz = xx % 4, yy % 4, zz % 8
        return ((xx // 2) * 8 + zz, yy * 4 + (xx % 2) * 2 + cc)

    def shard_columns(slot, q):
        j = q * 8 + (z + OFFSET[slot] + 8) % 8
        return pl.ds(pl.multiple_of(j * depth, depth), depth)

    def remote(src, dst, send, recv, target):
        return pltpu.make_async_remote_copy(
            src_ref=src, dst_ref=dst, send_sem=send, recv_sem=recv, device_id=target,
            device_id_type=MESH,
        )

    up, down = device(x, y, z + 1, c), device(x, y, z + 7, c)
    sibling = device(x, y, z, 1 - c)
    native = c == x_hi

    barrier = pltpu.get_barrier_semaphore()

    def greet(r, carry):
        pl.semaphore_signal(
            barrier, inc=1, device_id=device(x + r % 4, y + r // 4, z, c), device_id_type=MESH
        )
        return carry

    greeted = [(x, y, z + dz, cc) for dz in (1, 7) for cc in range(2)]
    greeted += [(x, y, z, 1 - c), (x + 2, y, z, 1 - c)]
    for other in [device(*there) for there in greeted]:
        pl.semaphore_signal(barrier, inc=1, device_id=other, device_id_type=MESH)
    lax.fori_loop(1, PEERS, greet, 0)

    fetch = pltpu.make_async_copy(tok_hbm, tok, tok_sem.at[0])
    fetch.start()

    near, far = x_hi, 1 - x_hi
    sources = (wg.at[0], wu.at[0])
    half = depth // HALVES

    def rows_of(h):
        return pl.ds(h * half, half)

    for k in range(2):
        for h in range(HALVES):
            start = pltpu.make_async_copy
            part = sources[k].at[rows_of(h)], wgu.at[k, 0, near, rows_of(h)]

            @pl.when(native & (c == k))
            def _():
                start(*part, own_recv.at[near, 0, h]).start()

            @pl.when(native & (c != k))
            def _():
                start(*part, pair_recv.at[near, 0, h]).start()

    @pl.when(native)
    def _():
        pltpu.make_async_copy(wd.at[0], wdn.at[0, c], down_recv.at[0]).start()

    eye = lax.broadcasted_iota(jnp.int32, (per, per), 0) == lax.broadcasted_iota(
        jnp.int32, (per, per), 1
    )
    token_id = lax.broadcasted_iota(jnp.int32, (per, onehot.shape[1]), 1).astype(jnp.float32)
    for r in range(PEERS):
        xx, yy = (x + r % 4) % 4, (y + r // 4) % 4
        e = yy * 4 + (xx % 2) * 2 + xx // 2
        picks = cho[0, pl.ds(e, 1), :].astype(jnp.float32)
        weights = gat[0, pl.ds(e, 1), :]
        pick_col = jnp.sum(jnp.where(eye, picks, 0.0), axis=1, keepdims=True)
        gate_col = jnp.sum(jnp.where(eye, weights, 0.0), axis=1, keepdims=True)
        hit = token_id == pick_col
        onehot[pl.ds(r * per, per), :] = jnp.where(hit, 1.0, 0.0).astype(jnp.bfloat16)
        gcol[pl.ds(r * per, per), :] = jnp.where(hit, gate_col, 0.0)

    pl.semaphore_wait(barrier, PEERS - 1 + len(greeted))

    def near_first(k, h, there):
        slot, index = (2, 0) if there == 1 else (1, 1)
        return remote(
            sources[k].at[rows_of(h)], wgu.at[k, slot, near, rows_of(h)],
            first_send.at[index, k, h], own_recv.at[near, slot, h], device(x, y, z + there, k),
        )

    def near_sibling(k, h, semaphores):
        return remote(
            sources[k].at[rows_of(h)], wgu.at[k, 0, near, rows_of(h)],
            first_send.at[2, k, h], semaphores.at[near, 0, h], sibling,
        )

    def far_first(k, h):
        return remote(
            sources[k].at[rows_of(h)], wgu.at[k, 0, x_hi, rows_of(h)],
            first_send.at[0, k, h], own_recv.at[x_hi, 0, h], device(x + 2, y, z, k),
        )

    def near_firsts(act):
        for h in range(HALVES):
            for k in range(2):
                act(near_first(k, h, 1))
                act(near_first(k, h, 7))
        for h in range(HALVES):
            for k in range(2):

                @pl.when(c == k)
                def _():
                    act(near_sibling(k, h, pair_recv))

                @pl.when(c != k)
                def _():
                    act(near_sibling(k, h, own_recv))

    def far_firsts(act):
        for h in range(HALVES):
            for k in range(2):
                act(far_first(k, h))

    def far_down():
        return remote(
            wd.at[0], wdn.at[0, 1 - c], far_send.at[0], down_recv.at[0],
            device(x + 2, y, z, 1 - c),
        )

    @pl.when(native)
    def _():
        near_firsts(lambda copy: copy.start())

    @pl.when(jnp.logical_not(native))
    def _():
        far_firsts(lambda copy: copy.start())

    def arrived(slot, q, h):
        part = wgu.at[c, slot, q, rows_of(h)]
        pltpu.make_async_copy(part, part, own_recv.at[q, slot, h]).wait()

    def pair(slot, q, h):
        part = wgu.at[c, slot, q, rows_of(h)]
        return remote(part, part, pair_send.at[q, slot, h], pair_recv.at[q, slot, h], sibling)

    def from_pair(slot, q, h):
        part = wgu.at[1 - c, slot, q, rows_of(h)]
        pltpu.make_async_copy(part, part, pair_recv.at[q, slot, h]).wait()

    def hop(src, dst, q, h, target):
        return remote(
            wgu.at[c, src, q, rows_of(h)], wgu.at[c, dst, q, rows_of(h)], own_send.at[q, dst, h],
            own_recv.at[q, dst, h], target,
        )

    def down_arrived(slot):
        part = wdn.at[slot, c]
        pltpu.make_async_copy(part, part, down_recv.at[slot]).wait()

    def swap(slot):
        part = wdn.at[slot, c]
        return remote(part, part, swap_send.at[slot], swap_recv.at[slot], sibling)

    def from_swap(slot):
        part = wdn.at[slot, 1 - c]
        pltpu.make_async_copy(part, part, swap_recv.at[slot]).wait()

    def down_hop(src, dst, target):
        return remote(
            wdn.at[src, c], wdn.at[dst, c], down_send.at[dst], down_recv.at[dst], target
        )

    last_src, last_target = 6 - c, device(x, y, z + 1 + 6 * c, c)

    def onward(slot, send):
        if slot == 0:
            send(0, 2, up)
            send(0, 1, down)
        elif slot in (1, 3):
            send(slot, slot + 2, down)
        elif slot in (2, 4):
            send(slot, slot + 2, up)
        elif slot in (5, 6):

            @pl.when(last_src == slot)
            def _():
                send(slot, 7, last_target)

    def spread(slot, q, h):
        arrived(slot, q, h)
        onward(slot, lambda src, dst, target: hop(src, dst, q, h, target).start())
        pair(slot, q, h).start()

    def columns(group):
        return pl.ds(group[0] * wide, len(group) * wide)

    def token_block(ref, group, r):
        return ref.at[pl.ds(pl.multiple_of(r * per, per), per), columns(group)]

    def send_tokens(g):
        group = GROUPS[g]
        for slot in group:
            for q in range(2):
                stage[:, pl.ds(slot * wide + q * depth, depth)] = jnp.dot(
                    onehot[...], tok[:, shard_columns(slot, q)], preferred_element_type=jnp.float32
                ).astype(jnp.bfloat16)

        def send(r, carry):
            remote(
                token_block(stage, group, r), token_block(xin, group, r), tok_send.at[g],
                tok_recv.at[g], device(x + r % 4, y + r // 4, z, c),
            ).start()
            return carry

        lax.fori_loop(1, PEERS, send, 0)
        xin[pl.ds(0, per), columns(group)] = stage[pl.ds(0, per), columns(group)]

    def spread_group(g, q, h):
        for slot in GROUPS[g]:
            spread(slot, q, h)

    fetch.wait()
    send_tokens(0)
    spread_group(0, far, 0)
    spread_group(1, near, 0)
    send_tokens(1)
    spread_group(0, far, 1)
    spread_group(1, near, 1)
    for g in range(2, len(GROUPS)):
        send_tokens(g)

    @pl.when(jnp.logical_not(native))
    def _():
        far_down().start()

    mixed = gcol[...].T
    high = mixed.astype(jnp.bfloat16)
    gmix[0] = high
    gmix[1] = (mixed - high.astype(jnp.float32)).astype(jnp.bfloat16)

    others = pl.ds(per, rows - per)

    def products_ready(g):
        group = GROUPS[g]
        for q in (near, far):
            for slot in group:
                for h in range(HALVES):
                    from_pair(slot, q, h)
        if g == 0:
            for h in range(HALVES):
                arrived(0, near, h)
        block = xin.at[others, columns(group)]
        pltpu.make_async_copy(block, block, tok_recv.at[g]).wait()

    def product(g, k, lanes):
        group = GROUPS[g]
        part = wgu[k, pl.ds(group[0], len(group)), :, :, lanes]
        return jnp.dot(
            xin[:, columns(group)], part.reshape(len(group) * wide, 256),
            preferred_element_type=jnp.float32,
        )

    def add_products(g):
        products_ready(g)

        def multiply(n, carry):
            k, tile = n // tiles, n % tiles
            more = product(g, k, pl.ds(pl.multiple_of(tile * 256, 256), 256))
            if g == 0:
                acc[n] = more
            else:
                acc[n] += more
            return carry

        lax.fori_loop(0, 2 * tiles, multiply, 0)

    def make_hidden(g):
        products_ready(g)
        for tile in range(tiles):
            lanes = pl.ds(tile * 256, 256)
            gate_part = acc[tile] + product(g, 0, lanes)
            up_part = acc[tiles + tile] + product(g, 1, lanes)
            hid[:, lanes] = (gate_part / (1.0 + jnp.exp(-gate_part)) * up_part).astype(jnp.bfloat16)

    ready = {(2, 1): 0, (3, 0): 1, (3, 1): 2}
    for g in range(2, len(GROUPS)):
        for h in range(HALVES):
            spread_group(g - 1, far, h)
            spread_group(g, near, h)
            if (g, h) in ready:
                add_products(ready[g, h])
    add_products(3)
    for h in range(HALVES):
        spread_group(4, far, h)
        if h == 0:
            down_arrived(0)
            onward(0, lambda src, dst, target: down_hop(src, dst, target).start())
            swap(0).start()
    make_hidden(4)

    for slot in range(SLOTS):
        for fresh in next((g for g in GROUPS[1:] if g[0] == slot), ()):
            down_arrived(fresh)
            onward(fresh, lambda src, dst, target: down_hop(src, dst, target).start())
            swap(fresh).start()
        from_swap(slot)
        for q in range(2):
            ost[slot, :, pl.ds(q * depth, depth)] = jnp.dot(
                hid[...], wdn[slot, q], preferred_element_type=jnp.float32
            ).astype(jnp.bfloat16)

        def give_back(r, carry):
            block = pl.ds(pl.multiple_of(r * per, per), per)
            remote(
                ost.at[slot, block], ret.at[slot, block], ret_send.at[slot], ret_recv.at[slot],
                device(x + 4 - r % 4, y + 4 - r // 4, z, c),
            ).start()
            return carry

        lax.fori_loop(1, PEERS, give_back, 0)
        ret[slot, pl.ds(0, per), :] = ost[slot, pl.ds(0, per), :]

    for slot in range(SLOTS):
        block = ret.at[slot, others]
        pltpu.make_async_copy(block, block, ret_recv.at[slot]).wait()
        for q in range(2):
            part = ret[slot, :, pl.ds(q * depth, depth)]
            o[:, shard_columns(slot, q)] = (
                jnp.dot(gmix[0], part, preferred_element_type=jnp.float32)
                + jnp.dot(gmix[1], part, preferred_element_type=jnp.float32)
            ).astype(jnp.bfloat16)

    for g, group in enumerate(GROUPS):
        block = stage.at[others, columns(group)]
        pltpu.make_async_copy(block, block, tok_send.at[g]).wait()
    for slot in range(SLOTS):
        block = ost.at[slot, others]
        pltpu.make_async_copy(block, block, ret_send.at[slot]).wait()
        swap(slot).wait_send()
        for h in range(HALVES):
            for q in (near, far):
                if slot > 0 or q is far:
                    pair(slot, q, h).wait_send()
                if slot > 2 or (slot > 0 and q is far):
                    hop(0, slot, q, h, up).wait_send()
        if slot > 0:
            down_hop(0, slot, up).wait_send()
    @pl.when(native)
    def _():
        near_firsts(lambda copy: copy.wait_send())

    @pl.when(jnp.logical_not(native))
    def _():
        far_firsts(lambda copy: copy.wait_send())
        far_down().wait_send()


def shards(tokens, chosen, gates, w_gate, w_up, w_down):
    count, width = tokens.shape
    per = chosen.shape[2]
    rows = PEERS * per
    depth, hidden = w_gate.shape[1:]
    vmem = pl.BlockSpec(memory_space=pltpu.VMEM)
    hbm = pl.BlockSpec(memory_space=pl.ANY)
    bf16, f32 = jnp.bfloat16, jnp.float32
    dma = pltpu.SemaphoreType.DMA
    return pl.pallas_call(
        moe_kernel,
        out_shape=pltpu.VMEM((count, width), bf16),
        in_specs=[hbm, vmem, vmem, hbm, hbm, hbm],
        out_specs=vmem,
        scratch_shapes=[
            pltpu.VMEM((count, width), bf16),
            pltpu.VMEM((rows, count), bf16),
            pltpu.VMEM((rows, count), f32),
            pltpu.VMEM((2, count, rows), bf16),
            pltpu.VMEM((rows, width), bf16),
            pltpu.VMEM((rows, width), bf16),
            pltpu.VMEM((2, SLOTS, 2, depth, hidden), bf16),
            pltpu.VMEM((SLOTS, 2, hidden, depth), bf16),
            pltpu.VMEM((2 * hidden // 256, rows, 256), f32),
            pltpu.VMEM((rows, hidden), bf16),
            pltpu.VMEM((SLOTS, rows, width // SLOTS), bf16),
            pltpu.VMEM((SLOTS, rows, width // SLOTS), bf16),
            dma((1,)),
            dma((len(GROUPS),)),
            dma((len(GROUPS),)),
            dma((SLOTS,)),
            dma((SLOTS,)),
            dma((2, SLOTS, HALVES)),
            dma((2, SLOTS, HALVES)),
            dma((2, SLOTS, HALVES)),
            dma((2, SLOTS, HALVES)),
            dma((SLOTS,)),
            dma((SLOTS,)),
            dma((SLOTS,)),
            dma((SLOTS,)),
            dma((3, 2, HALVES)),
            dma((1,)),
        ],
        compiler_params=pltpu.CompilerParams(
            collective_id=0, has_side_effects=True, vmem_limit_bytes=61 * 2**20
        ),
        cost_estimate=pl.CostEstimate(
            flops=11 * 10**9, bytes_accessed=8 * 2**20, transcendentals=rows * hidden
        ),
        name="moe",
    )(tokens, chosen, gates, w_gate, w_up, w_down)


def solution(mesh):
    in_specs = (
        P(("dp", "expert"), None),
        P(("dp", "expert"), None, None),
        P(("dp", "expert"), None, None),
        P("expert", "dp", None),
        P("expert", "dp", None),
        P("expert", None, "dp"),
    )
    out_specs = P(("dp", "expert"), None)
    return jax.shard_map(shards, mesh=mesh, in_specs=in_specs, out_specs=out_specs, check_vma=False)
```

```python
import jax
import jax.numpy as jnp
from jax import lax
from jax.experimental import pallas as pl
from jax.experimental.pallas import tpu as pltpu
from jax.sharding import PartitionSpec as P

MESH = pl.DeviceIdType.MESH
OFFSET = (0, 1, -1, 2, -2, 3, -3, 4)
PEERS = 16
SLOTS = 8
HALVES = 2
GROUPS = ((0,), (1, 2), (3, 4), (5, 6), (7,))


def moe_kernel(
    tok_hbm, cho, gat, wg, wu, wd, o,
    tok, onehot, gcol, gmix, stage, xin, wgu, wdn, acc, hid, ost, ret,
    tok_sem, tok_send, tok_recv, ret_send, ret_recv,
    own_recv, own_send, pair_recv, pair_send, down_recv, down_send, swap_recv, swap_send, first_send, far_send,
):
    dp, ex = lax.axis_index("dp"), lax.axis_index("expert")
    x_hi, z = dp // 8, dp % 8
    y, x_lo, c = ex // 4, (ex // 2) % 2, ex % 2
    x = x_hi * 2 + x_lo
    per = cho.shape[2]
    rows = PEERS * per
    depth, hidden = wg.shape[1:]
    tiles = hidden // 256
    wide = 2 * depth

    def device(xx, yy, zz, cc):
        xx, yy, zz = xx % 4, yy % 4, zz % 8
        return ((xx // 2) * 8 + zz, yy * 4 + (xx % 2) * 2 + cc)

    def shard_columns(slot, q):
        j = q * 8 + (z + OFFSET[slot] + 8) % 8
        return pl.ds(pl.multiple_of(j * depth, depth), depth)

    def remote(src, dst, send, recv, target):
        return pltpu.make_async_remote_copy(
            src_ref=src, dst_ref=dst, send_sem=send, recv_sem=recv, device_id=target,
            device_id_type=MESH,
        )

    up, down = device(x, y, z + 1, c), device(x, y, z + 7, c)
    sibling = device(x, y, z, 1 - c)
    native = c == x_hi

    barrier = pltpu.get_barrier_semaphore()

    def greet(r, carry):
        pl.semaphore_signal(
            barrier, inc=1, device_id=device(x + r % 4, y + r // 4, z, c), device_id_type=MESH
        )
        return carry

    greeted = [(x, y, z + dz, cc) for dz in (1, 7) for cc in range(2)]
    greeted += [(x, y, z, 1 - c), (x + 2, y, z, 1 - c)]
    for other in [device(*there) for there in greeted]:
        pl.semaphore_signal(barrier, inc=1, device_id=other, device_id_type=MESH)
    lax.fori_loop(1, PEERS, greet, 0)

    fetch = pltpu.make_async_copy(tok_hbm, tok, tok_sem.at[0])
    fetch.start()

    near, far = x_hi, 1 - x_hi
    sources = (wg.at[0], wu.at[0])
    half = depth // HALVES

    def rows_of(h):
        return pl.ds(h * half, half)

    for k in range(2):
        for h in range(HALVES):
            start = pltpu.make_async_copy
            part = sources[k].at[rows_of(h)], wgu.at[k, 0, near, rows_of(h)]

            @pl.when(native & (c == k))
            def _():
                start(*part, own_recv.at[near, 0, h]).start()

            @pl.when(native & (c != k))
            def _():
                start(*part, pair_recv.at[near, 0, h]).start()

    @pl.when(native)
    def _():
        pltpu.make_async_copy(wd.at[0], wdn.at[0, c], down_recv.at[0]).start()

    eye = lax.broadcasted_iota(jnp.int32, (per, per), 0) == lax.broadcasted_iota(
        jnp.int32, (per, per), 1
    )
    token_id = lax.broadcasted_iota(jnp.int32, (per, onehot.shape[1]), 1).astype(jnp.float32)
    for r in range(PEERS):
        xx, yy = (x + r % 4) % 4, (y + r // 4) % 4
        e = yy * 4 + (xx % 2) * 2 + xx // 2
        picks = cho[0, pl.ds(e, 1), :].astype(jnp.float32)
        weights = gat[0, pl.ds(e, 1), :]
        pick_col = jnp.sum(jnp.where(eye, picks, 0.0), axis=1, keepdims=True)
        gate_col = jnp.sum(jnp.where(eye, weights, 0.0), axis=1, keepdims=True)
        hit = token_id == pick_col
        onehot[pl.ds(r * per, per), :] = jnp.where(hit, 1.0, 0.0).astype(jnp.bfloat16)
        gcol[pl.ds(r * per, per), :] = jnp.where(hit, gate_col, 0.0)

    pl.semaphore_wait(barrier, PEERS - 1 + len(greeted))

    def near_first(k, h, there):
        slot, index = (2, 0) if there == 1 else (1, 1)
        return remote(
            sources[k].at[rows_of(h)], wgu.at[k, slot, near, rows_of(h)],
            first_send.at[index, k, h], own_recv.at[near, slot, h], device(x, y, z + there, k),
        )

    def near_sibling(k, h, semaphores):
        return remote(
            sources[k].at[rows_of(h)], wgu.at[k, 0, near, rows_of(h)],
            first_send.at[2, k, h], semaphores.at[near, 0, h], sibling,
        )

    def far_first(k, h):
        return remote(
            sources[k].at[rows_of(h)], wgu.at[k, 0, x_hi, rows_of(h)],
            first_send.at[0, k, h], own_recv.at[x_hi, 0, h], device(x + 2, y, z, k),
        )

    def near_firsts(act):
        for h in range(HALVES):
            for k in range(2):
                act(near_first(k, h, 1))
                act(near_first(k, h, 7))
        for h in range(HALVES):
            for k in range(2):

                @pl.when(c == k)
                def _():
                    act(near_sibling(k, h, pair_recv))

                @pl.when(c != k)
                def _():
                    act(near_sibling(k, h, own_recv))

    def far_firsts(act):
        for h in range(HALVES):
            for k in range(2):
                act(far_first(k, h))

    def far_down():
        return remote(
            wd.at[0], wdn.at[0, 1 - c], far_send.at[0], down_recv.at[0],
            device(x + 2, y, z, 1 - c),
        )

    @pl.when(native)
    def _():
        near_firsts(lambda copy: copy.start())

    @pl.when(jnp.logical_not(native))
    def _():
        far_firsts(lambda copy: copy.start())

    def arrived(slot, q, h):
        part = wgu.at[c, slot, q, rows_of(h)]
        pltpu.make_async_copy(part, part, own_recv.at[q, slot, h]).wait()

    def pair(slot, q, h):
        part = wgu.at[c, slot, q, rows_of(h)]
        return remote(part, part, pair_send.at[q, slot, h], pair_recv.at[q, slot, h], sibling)

    def from_pair(slot, q, h):
        part = wgu.at[1 - c, slot, q, rows_of(h)]
        pltpu.make_async_copy(part, part, pair_recv.at[q, slot, h]).wait()

    def hop(src, dst, q, h, target):
        return remote(
            wgu.at[c, src, q, rows_of(h)], wgu.at[c, dst, q, rows_of(h)], own_send.at[q, dst, h],
            own_recv.at[q, dst, h], target,
        )

    def down_arrived(slot):
        part = wdn.at[slot, c]
        pltpu.make_async_copy(part, part, down_recv.at[slot]).wait()

    def swap(slot):
        part = wdn.at[slot, c]
        return remote(part, part, swap_send.at[slot], swap_recv.at[slot], sibling)

    def from_swap(slot):
        part = wdn.at[slot, 1 - c]
        pltpu.make_async_copy(part, part, swap_recv.at[slot]).wait()

    def down_hop(src, dst, target):
        return remote(
            wdn.at[src, c], wdn.at[dst, c], down_send.at[dst], down_recv.at[dst], target
        )

    last_src, last_target = 6 - c, device(x, y, z + 1 + 6 * c, c)

    def onward(slot, send):
        if slot == 0:
            send(0, 2, up)
            send(0, 1, down)
        elif slot in (1, 3):
            send(slot, slot + 2, down)
        elif slot in (2, 4):
            send(slot, slot + 2, up)
        elif slot in (5, 6):

            @pl.when(last_src == slot)
            def _():
                send(slot, 7, last_target)

    def spread(slot, q, h):
        arrived(slot, q, h)
        onward(slot, lambda src, dst, target: hop(src, dst, q, h, target).start())
        pair(slot, q, h).start()

    def columns(group):
        return pl.ds(group[0] * wide, len(group) * wide)

    def token_block(ref, group, r):
        return ref.at[pl.ds(pl.multiple_of(r * per, per), per), columns(group)]

    def send_tokens(g):
        group = GROUPS[g]
        for slot in group:
            for q in range(2):
                stage[:, pl.ds(slot * wide + q * depth, depth)] = jnp.dot(
                    onehot[...], tok[:, shard_columns(slot, q)], preferred_element_type=jnp.float32
                ).astype(jnp.bfloat16)

        def send(r, carry):
            remote(
                token_block(stage, group, r), token_block(xin, group, r), tok_send.at[g],
                tok_recv.at[g], device(x + r % 4, y + r // 4, z, c),
            ).start()
            return carry

        lax.fori_loop(1, PEERS, send, 0)
        xin[pl.ds(0, per), columns(group)] = stage[pl.ds(0, per), columns(group)]

    def spread_group(g, q, h):
        for slot in GROUPS[g]:
            spread(slot, q, h)

    fetch.wait()
    send_tokens(0)
    spread_group(0, far, 0)
    spread_group(1, near, 0)
    send_tokens(1)
    spread_group(0, far, 1)
    spread_group(1, near, 1)
    for g in range(2, len(GROUPS)):
        send_tokens(g)

    @pl.when(jnp.logical_not(native))
    def _():
        far_down().start()

    others = pl.ds(per, rows - per)

    def products_ready(g):
        group = GROUPS[g]
        for q in (near, far):
            for slot in group:
                for h in range(HALVES):
                    from_pair(slot, q, h)
        if g == 0:
            for h in range(HALVES):
                arrived(0, near, h)
        block = xin.at[others, columns(group)]
        pltpu.make_async_copy(block, block, tok_recv.at[g]).wait()

    def product(g, k, lanes):
        group = GROUPS[g]
        part = wgu[k, pl.ds(group[0], len(group)), :, :, lanes]
        return jnp.dot(
            xin[:, columns(group)], part.reshape(len(group) * wide, 256),
            preferred_element_type=jnp.float32,
        )

    def add_products(g):
        products_ready(g)

        def multiply(n, carry):
            k, tile = n // tiles, n % tiles
            more = product(g, k, pl.ds(pl.multiple_of(tile * 256, 256), 256))
            if g == 0:
                acc[n] = more
            else:
                acc[n] += more
            return carry

        lax.fori_loop(0, 2 * tiles, multiply, 0)

    def make_hidden(g):
        products_ready(g)
        for tile in range(tiles):
            lanes = pl.ds(tile * 256, 256)
            gate_part = acc[tile] + product(g, 0, lanes)
            up_part = acc[tiles + tile] + product(g, 1, lanes)
            hid[:, lanes] = (gate_part / (1.0 + jnp.exp(-gate_part)) * up_part).astype(jnp.bfloat16)

    ready = {(2, 1): 0, (3, 0): 1, (3, 1): 2}
    for g in range(2, len(GROUPS)):
        for h in range(HALVES):
            spread_group(g - 1, far, h)
            spread_group(g, near, h)
            if (g, h) in ready:
                add_products(ready[g, h])
    add_products(3)
    for h in range(HALVES):
        spread_group(4, far, h)
        if h == 0:
            down_arrived(0)
            onward(0, lambda src, dst, target: down_hop(src, dst, target).start())
            swap(0).start()
    make_hidden(4)

    for slot in range(SLOTS):
        for fresh in next((g for g in GROUPS[1:] if g[0] == slot), ()):
            down_arrived(fresh)
            onward(fresh, lambda src, dst, target: down_hop(src, dst, target).start())
            swap(fresh).start()
        from_swap(slot)
        for q in range(2):
            ost[slot, :, pl.ds(q * depth, depth)] = jnp.dot(
                hid[...], wdn[slot, q], preferred_element_type=jnp.float32
            ).astype(jnp.bfloat16)

        def give_back(r, carry):
            block = pl.ds(pl.multiple_of(r * per, per), per)
            remote(
                ost.at[slot, block], ret.at[slot, block], ret_send.at[slot], ret_recv.at[slot],
                device(x + 4 - r % 4, y + 4 - r // 4, z, c),
            ).start()
            return carry

        lax.fori_loop(1, PEERS, give_back, 0)
        ret[slot, pl.ds(0, per), :] = ost[slot, pl.ds(0, per), :]

    mixed = gcol[...].T
    high = mixed.astype(jnp.bfloat16)
    gmix[0] = high
    gmix[1] = (mixed - high.astype(jnp.float32)).astype(jnp.bfloat16)

    for slot in range(SLOTS):
        block = ret.at[slot, others]
        pltpu.make_async_copy(block, block, ret_recv.at[slot]).wait()
        for q in range(2):
            part = ret[slot, :, pl.ds(q * depth, depth)]
            o[:, shard_columns(slot, q)] = (
                jnp.dot(gmix[0], part, preferred_element_type=jnp.float32)
                + jnp.dot(gmix[1], part, preferred_element_type=jnp.float32)
            ).astype(jnp.bfloat16)

    for g, group in enumerate(GROUPS):
        block = stage.at[others, columns(group)]
        pltpu.make_async_copy(block, block, tok_send.at[g]).wait()
    for slot in range(SLOTS):
        block = ost.at[slot, others]
        pltpu.make_async_copy(block, block, ret_send.at[slot]).wait()
        swap(slot).wait_send()
        for h in range(HALVES):
            for q in (near, far):
                if slot > 0 or q is far:
                    pair(slot, q, h).wait_send()
                if slot > 2 or (slot > 0 and q is far):
                    hop(0, slot, q, h, up).wait_send()
        if slot > 0:
            down_hop(0, slot, up).wait_send()
    @pl.when(native)
    def _():
        near_firsts(lambda copy: copy.wait_send())

    @pl.when(jnp.logical_not(native))
    def _():
        far_firsts(lambda copy: copy.wait_send())
        far_down().wait_send()


def shards(tokens, chosen, gates, w_gate, w_up, w_down):
    count, width = tokens.shape
    per = chosen.shape[2]
    rows = PEERS * per
    depth, hidden = w_gate.shape[1:]
    vmem = pl.BlockSpec(memory_space=pltpu.VMEM)
    hbm = pl.BlockSpec(memory_space=pl.ANY)
    bf16, f32 = jnp.bfloat16, jnp.float32
    dma = pltpu.SemaphoreType.DMA
    return pl.pallas_call(
        moe_kernel,
        out_shape=pltpu.VMEM((count, width), bf16),
        in_specs=[hbm, vmem, vmem, hbm, hbm, hbm],
        out_specs=vmem,
        scratch_shapes=[
            pltpu.VMEM((count, width), bf16),
            pltpu.VMEM((rows, count), bf16),
            pltpu.VMEM((rows, count), f32),
            pltpu.VMEM((2, count, rows), bf16),
            pltpu.VMEM((rows, width), bf16),
            pltpu.VMEM((rows, width), bf16),
            pltpu.VMEM((2, SLOTS, 2, depth, hidden), bf16),
            pltpu.VMEM((SLOTS, 2, hidden, depth), bf16),
            pltpu.VMEM((2 * hidden // 256, rows, 256), f32),
            pltpu.VMEM((rows, hidden), bf16),
            pltpu.VMEM((SLOTS, rows, width // SLOTS), bf16),
            pltpu.VMEM((SLOTS, rows, width // SLOTS), bf16),
            dma((1,)),
            dma((len(GROUPS),)),
            dma((len(GROUPS),)),
            dma((SLOTS,)),
            dma((SLOTS,)),
            dma((2, SLOTS, HALVES)),
            dma((2, SLOTS, HALVES)),
            dma((2, SLOTS, HALVES)),
            dma((2, SLOTS, HALVES)),
            dma((SLOTS,)),
            dma((SLOTS,)),
            dma((SLOTS,)),
            dma((SLOTS,)),
            dma((3, 2, HALVES)),
            dma((1,)),
        ],
        compiler_params=pltpu.CompilerParams(
            collective_id=0, has_side_effects=True, vmem_limit_bytes=61 * 2**20
        ),
        cost_estimate=pl.CostEstimate(
            flops=11 * 10**9, bytes_accessed=8 * 2**20, transcendentals=rows * hidden
        ),
        name="moe",
    )(tokens, chosen, gates, w_gate, w_up, w_down)


def solution(mesh):
    in_specs = (
        P(("dp", "expert"), None),
        P(("dp", "expert"), None, None),
        P(("dp", "expert"), None, None),
        P("expert", "dp", None),
        P("expert", "dp", None),
        P("expert", None, "dp"),
    )
    out_specs = P(("dp", "expert"), None)
    return jax.shard_map(shards, mesh=mesh, in_specs=in_specs, out_specs=out_specs, check_vma=False)
```
